512 devices in a mesh: group: 16 (over z, core), dom: 32 (over x, y).
Axes of the slice: x: 4, y: 8, z: 8, core: 2. Of those that a mesh axis runs over, the one named last changes fastest.
Arguments:
- features: bfloat16 [196608, 512], P(('group', 'dom')), may hold values from -6 to 6
- w_self: bfloat16 [512, 512], replicated, may hold values from -0.25 to 0.25
- w_neigh: bfloat16 [512, 512], replicated, may hold values from -0.25 to 0.25
- bias_term: float32 [512], replicated, may hold values from -3 to 3
- degree: int32 [196608], P(('group', 'dom')), may hold values from 4 to 32
- local_adj: int32 [196608, 384], P(('group', 'dom')), may hold values 0 or 1
- hub_adj: int32 [196608, 512], P(('group', 'dom')), may hold values 0 or 1
- hub_rows: int32 [512, 1], P(('group', 'dom')), may hold values from 0 to 383
- remote_adj: int32 [196608, 256], P(('group', 'dom')), may hold values 0 or 1
- send_rows: int32 [512, 32, 8], P(('group', 'dom')), may hold values from 0 to 383
- send_counts: int32 [512, 32], P(('group', 'dom')), may hold values from 0 to 8, as said below
- grad_out: bfloat16 [196608, 512], P(('group', 'dom')), may hold values from -6 to 6
Outputs:
- out_feats: bfloat16 [196608, 512], P(('group', 'dom'))
- grad_features: bfloat16 [196608, 512], P(('group', 'dom'))
- hub_grad: float32 [512, 512], P(('group', 'dom'))
The draws below stay inside these ranges and needn't reach their ends.
Inputs may be any that keep to these rules, and one draw needn't show every extreme that they name: send_counts[p, j] live slots are the first ones of send_rows[p, j]; a device sends nothing to itself (entry j equal to its own index along dom is 0); in every group some device receives 8 live rows from every other device of the group. send_rows[p, j, s] is a local row of device p; rows may repeat. Hub number p * 1 + k is local row hub_rows[p, k] of device p.
All inputs are finite; a program needn't handle non-finite values. No bound on the sum of `local_adj` or of `hub_adj` or of `remote_adj` on one device may be relied on, other than what follows from the above.
Results may differ from the reference program's by a relative error of at most 0.014.
Values may be sent and summed in bfloat16 or wider, within the bound.
No kernel may reach another device: no remote copies, remote signals or barrier semaphores. Data moves between devices by JAX's collectives and lax.ppermute only.
A program may use at most 64 MiB of HBM per device.

```python
import jax
import jax.numpy as jnp
from jax import lax

D = 512
NODE_DEV = 384
HUB_DEV = 1
SLOT = 8
DEVS = 512
PEERS = 32
NODES = 196608
HUBS = 512
RECV = 256


def draw_send_counts(key, part):
    first, second = jax.random.split(key)
    counts = jax.random.randint(first, (DEVS, PEERS), 1, SLOT + 1)
    full = jax.random.randint(second, (DEVS // PEERS, 1), 0, PEERS)
    full_rows = jnp.repeat(full, PEERS, axis=0)
    target = jnp.arange(PEERS, dtype=jnp.int32)[None, :]
    source = (jnp.arange(DEVS, dtype=jnp.int32) % PEERS)[:, None]
    counts = jnp.where(target == full_rows, SLOT, counts)
    counts = jnp.where(target == source, 0, counts)
    return counts.astype(jnp.int32)


def place_ends(entries, key, least, high):
    place = [jax.random.randint(jax.random.fold_in(key, axis), (), 0, length) for axis, length in enumerate(entries.shape)]
    main_axis = entries.shape.index(max(entries.shape))
    beside = place[:main_axis] + [(place[main_axis] + 1) % entries.shape[main_axis]] + place[main_axis + 1:]
    return entries.at[tuple(place)].set(least).at[tuple(beside)].set(high)


def levels(stream_key, dims, pieces, low, top_value):
    gain, own = 1.0, jax.random.fold_in(stream_key, 6)
    for axis_at, shards_of in pieces:
        heights = jnp.exp(jax.random.uniform(jax.random.fold_in(own, axis_at), (shards_of,), jnp.float32, low / len(pieces), top_value / len(pieces)))
        gain = gain * jnp.repeat(heights, dims[axis_at] // shards_of).reshape([-1 if axis == axis_at else 1 for axis in range(len(dims))])
    return gain


def gaussian(stream_key, shape, deviation, bound, cuts=(), kind=jnp.bfloat16):
    values = deviation * jax.random.normal(stream_key, shape, jnp.float32)
    if cuts:
        values = values * levels(stream_key, shape, cuts, -0.22, 0.18)
    return jnp.clip(values, -bound, bound).astype(kind)


def setup_inputs(seed: int = 0) -> dict:
    key_of = jax.random.split(jax.random.key(seed), 13)
    features = gaussian(key_of[0], (NODES, D), 1.0, 6.0, ((0, 512),))
    w_self = gaussian(key_of[1], (D, D), D ** -0.5, 0.25)
    w_neigh = gaussian(key_of[2], (D, D), D ** -0.5, 0.25)
    bias_term = gaussian(key_of[3], (D,), 0.5, 3.0, (), jnp.float32)
    degree = place_ends(jax.random.randint(key_of[4], (NODES,), 4, 33), jax.random.fold_in(key_of[4], 1), 4, 32).astype(jnp.int32)
    local_adj = place_ends((jax.random.randint(key_of[5], (NODES, NODE_DEV), 0, 40) < 1).astype(jnp.int32), jax.random.fold_in(key_of[5], 1), 0, 1)
    hub_adj = place_ends((jax.random.randint(key_of[6], (NODES, HUBS), 0, 80) < 1).astype(jnp.int32), jax.random.fold_in(key_of[6], 1), 0, 1)
    hub_rows = place_ends(jax.random.randint(key_of[7], (DEVS, HUB_DEV), 0, NODE_DEV), jax.random.fold_in(key_of[7], 1), 0, NODE_DEV - 1).astype(jnp.int32)
    remote_adj = place_ends((jax.random.randint(key_of[8], (NODES, RECV), 0, 20) < 1).astype(jnp.int32), jax.random.fold_in(key_of[8], 1), 0, 1)
    send_rows = place_ends(jax.random.randint(key_of[9], (DEVS, PEERS, SLOT), 0, NODE_DEV), jax.random.fold_in(key_of[9], 1), 0, NODE_DEV - 1).astype(jnp.int32)
    send_counts = draw_send_counts(jax.random.fold_in(key_of[12], 71), 0)
    grad_out = gaussian(key_of[11], (NODES, D), 1.0, 6.0, ((0, 512),))
    return {"features": features, "w_self": w_self, "w_neigh": w_neigh, "bias_term": bias_term, "degree": degree, "local_adj": local_adj, "hub_adj": hub_adj, "hub_rows": hub_rows, "remote_adj": remote_adj, "send_rows": send_rows, "send_counts": send_counts, "grad_out": grad_out}


def transposed(matrix, other):
    return lax.dot_general(matrix, other, (((0,), (0,)), ((), ())), preferred_element_type=jnp.float32)


def back_product(grads, weight):
    return lax.dot_general(grads, weight, (((1,), (1,)), ((), ())), preferred_element_type=jnp.float32)


def reference(features, w_self, w_neigh, bias_term, degree, local_adj, hub_adj, hub_rows, remote_adj, send_rows, send_counts, grad_out):
    groups = DEVS // PEERS
    blocks = features.reshape(DEVS, NODE_DEV, D)
    hub_feats = jax.vmap(lambda block, index: block[index])(blocks, hub_rows).reshape(HUBS, D)
    picked = jax.vmap(lambda block, index: block[index])(blocks, send_rows)
    live_slots = jnp.arange(SLOT, dtype=jnp.int32)[None, None, :] < send_counts[:, :, None]
    sent = jnp.where(live_slots[..., None], picked, jnp.zeros((), picked.dtype))
    received = sent.reshape(groups, PEERS, PEERS, SLOT, D).swapaxes(1, 2).reshape(DEVS, RECV, D)

    def device_step(hub_total, inputs):
        block, local_part, hub_part, remote_part, incoming, degree_part, grad_part = inputs
        local_mat = local_part.astype(jnp.bfloat16)
        hub_mat = hub_part.astype(jnp.bfloat16)
        remote_mat = remote_part.astype(jnp.bfloat16)
        summed = block.astype(jnp.float32) + jnp.dot(local_mat, block, preferred_element_type=jnp.float32)
        summed = summed + jnp.dot(hub_mat, hub_feats, preferred_element_type=jnp.float32)
        summed = summed + jnp.dot(remote_mat, incoming, preferred_element_type=jnp.float32)
        denom = degree_part.astype(jnp.float32)[:, None] + 1.0
        mean_feats = (summed / denom).astype(jnp.bfloat16)
        preact = jnp.dot(block, w_self, preferred_element_type=jnp.float32)
        preact = preact + jnp.dot(mean_feats, w_neigh, preferred_element_type=jnp.float32) + bias_term
        out_part = jax.nn.elu(preact).astype(jnp.bfloat16)
        slope = jnp.where(preact > 0, 1.0, jnp.exp(jnp.minimum(preact, 0.0)))
        grad_pre = (grad_part.astype(jnp.float32) * slope).astype(jnp.bfloat16)
        back_self = back_product(grad_pre, w_self)
        grad_mean = (back_product(grad_pre, w_neigh) / denom).astype(jnp.bfloat16)
        grad_local = back_self + grad_mean.astype(jnp.float32) + transposed(local_mat, grad_mean)
        hub_total = hub_total + transposed(hub_mat, grad_mean)
        slot_grad = transposed(remote_mat, grad_mean).astype(jnp.bfloat16)
        return hub_total, (out_part, grad_local, slot_grad)

    inputs = (blocks, local_adj.reshape(DEVS, NODE_DEV, NODE_DEV), hub_adj.reshape(DEVS, NODE_DEV, HUBS),
              remote_adj.reshape(DEVS, NODE_DEV, RECV), received, degree.reshape(DEVS, NODE_DEV),
              grad_out.reshape(DEVS, NODE_DEV, D))
    hub_total, outputs = lax.scan(device_step, jnp.zeros((HUBS, D), jnp.float32), inputs)
    out_parts, grad_parts, slot_grads = outputs
    returned = slot_grads.reshape(groups, PEERS, PEERS, SLOT, D).swapaxes(1, 2).reshape(DEVS, PEERS, SLOT, D)
    returned = jnp.where(live_slots[..., None], returned, jnp.zeros((), returned.dtype)).astype(jnp.float32)
    hub_back = hub_total.reshape(DEVS, HUB_DEV, D)

    def owner_add(grad_part, rows_sent, back_rows, hub_index, hub_part):
        grad_part = grad_part.at[rows_sent.reshape(-1)].add(back_rows.reshape(RECV, D))
        return grad_part.at[hub_index].add(hub_part)

    grad_all = jax.vmap(owner_add)(grad_parts, send_rows, returned, hub_rows, hub_back)
    return out_parts.reshape(NODES, D), grad_all.astype(jnp.bfloat16).reshape(NODES, D), hub_total
```

```python
import jax
import jax.numpy as jnp
from jax import lax
from jax.sharding import Mesh
from jax.sharding import PartitionSpec as P

ALL = ("z", "core", "x", "y")
DOM = ("x", "y")
F32 = jnp.float32
BF16 = jnp.bfloat16


def matmul(lhs, rhs):
    return jnp.dot(lhs, rhs, preferred_element_type=F32)


def transposed(matrix, other):
    return lax.dot_general(matrix, other, (((0,), (0,)), ((), ())), preferred_element_type=F32)


def back_product(grads, weight):
    return lax.dot_general(grads, weight, (((1,), (1,)), ((), ())), preferred_element_type=F32)


def exchange(parts, axis):
    return lax.all_to_all(parts, axis, split_axis=0, concat_axis=0, tiled=True)


def on_device(
    features,
    w_self,
    w_neigh,
    bias_term,
    degree,
    local_adj,
    hub_adj,
    hub_rows,
    remote_adj,
    send_rows,
    send_counts,
    grad_out,
):
    nodes, width = features.shape
    n_z, n_core = lax.axis_size("z"), lax.axis_size("core")
    peers, slots = send_rows.shape[1:]
    hubs = hub_adj.shape[1]
    half = hubs // n_core
    my_core = lax.axis_index("core")

    hub_own = lax.dynamic_slice(features, (hub_rows[0, 0], 0), (1, width)).reshape(1, width // 128, 128)
    along_z = exchange(jnp.broadcast_to(hub_own, (n_z, width // 128, 128)), "z").reshape(n_z, width)

    live = jnp.arange(slots, dtype=jnp.int32)[None, :] < send_counts[0][:, None]
    picked = jnp.where(live, send_rows[0], -1).reshape(1, peers * slots)
    pick = (picked == jnp.arange(nodes, dtype=jnp.int32)[:, None]).astype(BF16)
    outgoing = transposed(pick, features).astype(BF16).reshape(peers, slots, width)
    payload = jnp.concatenate([outgoing, jnp.broadcast_to(along_z[None], (peers, n_z, width))], axis=1)
    incoming = exchange(payload, DOM)
    received = incoming[:, :slots].reshape(peers * slots, width)
    same_core = incoming[:, slots:].reshape(half, width)
    all_hubs = lax.all_gather(same_core, "core", axis=0, tiled=True)

    place = jnp.arange(hubs, dtype=jnp.int32)[None, :]
    at_core, at_peer, at_z = place // half, (place % half) // n_z, place % n_z
    source = (at_z * n_core + at_core) * peers + at_peer
    reorder = (source == jnp.arange(hubs, dtype=jnp.int32)[:, None]).astype(BF16)
    hub_mat = matmul(hub_adj.astype(BF16), reorder).astype(BF16)
    local_mat = local_adj.astype(BF16)
    remote_mat = remote_adj.astype(BF16)

    summed = features.astype(F32) + matmul(local_mat, features)
    summed = summed + matmul(hub_mat, all_hubs) + matmul(remote_mat, received)
    denom = degree.astype(F32)[:, None] + 1.0
    mean_feats = (summed / denom).astype(BF16)
    preact = matmul(features, w_self) + matmul(mean_feats, w_neigh) + bias_term
    low = jnp.minimum(preact, 0.0)
    out_feats = jnp.where(preact > 0, preact, jnp.expm1(low)).astype(BF16)
    slope = jnp.where(preact > 0, 1.0, jnp.exp(low))
    grad_pre = (grad_out.astype(F32) * slope).astype(BF16)
    grad_mean = (back_product(grad_pre, w_neigh) / denom).astype(BF16)

    hub_low, hub_high = hub_mat[:, :half], hub_mat[:, half:]
    mine = jnp.where(my_core == 0, hub_low, hub_high)
    other = jnp.where(my_core == 0, hub_high, hub_low)
    other_part = lax.ppermute(transposed(other, grad_mean).astype(BF16), "core", [(0, 1), (1, 0)])
    chip_part = (transposed(mine, grad_mean) + other_part.astype(F32)).astype(BF16)
    slot_grad = transposed(remote_mat, grad_mean).astype(BF16)
    payload = jnp.concatenate(
        [slot_grad.reshape(peers, slots, width), chip_part.reshape(peers, n_z, width)], axis=1
    )
    returned = exchange(payload, DOM)
    hub_z = jnp.sum(returned[:, slots:].astype(F32), axis=0)
    hub_parts = exchange(hub_z.reshape(n_z, width // 128, 128), "z")
    hub_grad = jnp.sum(hub_parts, axis=0).reshape(1, width)

    grad_local = back_product(grad_pre, w_self) + grad_mean.astype(F32) + transposed(local_mat, grad_mean)
    grad_local = grad_local + matmul(pick, returned[:, :slots].reshape(peers * slots, width))
    at_hub = jnp.arange(nodes, dtype=jnp.int32)[:, None] == hub_rows[0, 0]
    grad_features = (grad_local + jnp.where(at_hub, hub_grad, 0.0)).astype(BF16)
    return (out_feats, grad_features, hub_grad)


def solution(mesh):
    fine = Mesh(mesh.devices.reshape(8, 2, 4, 8), ALL)
    rows, whole = P(ALL), P()
    return jax.shard_map(
        on_device,
        mesh=fine,
        in_specs=(rows, whole, whole, whole, rows, rows, rows, rows, rows, rows, rows, rows),
        out_specs=(rows, rows, rows),
        check_vma=False,
    )
```

```python
import jax
import jax.numpy as jnp
from jax import lax
from jax.experimental import pallas as pl
from jax.experimental.pallas import tpu as pltpu
from jax.sharding import Mesh
from jax.sharding import PartitionSpec as P

ALL = ("z", "core", "x", "y")
DOM = ("x", "y")
F32 = jnp.float32
BF16 = jnp.bfloat16
LANES = 128
ROWS = 16
CORES, PEERS = 2, 32


def matmul(lhs, rhs):
    return jnp.dot(lhs, rhs, preferred_element_type=F32)


def transposed(matrix, other):
    return lax.dot_general(matrix, other, (((0,), (0,)), ((), ())), preferred_element_type=F32)


def back_product(grads, weight):
    return lax.dot_general(grads, weight, (((1,), (1,)), ((), ())), preferred_element_type=F32)


def exchange(parts, axis):
    return lax.all_to_all(parts, axis, split_axis=0, concat_axis=0, tiled=True)


def split_lanes(rows):
    parts = [rows[:, k : k + LANES] for k in range(0, rows.shape[1], LANES)]
    return jnp.stack(parts, axis=1)


def in_vmem(body, name, shapes, operands, flops, limit=8, untouched=0):
    spec = pl.BlockSpec(memory_space=pltpu.VMEM)
    moved = sum(x.size * x.dtype.itemsize for x in (*operands, *shapes)) if flops else 0
    return pl.pallas_call(
        body,
        out_shape=shapes,
        in_specs=[spec] * (len(operands) - untouched) + [pl.BlockSpec(memory_space=pl.ANY)] * untouched,
        out_specs=[spec] * len(shapes),
        compiler_params=pltpu.CompilerParams(vmem_limit_bytes=limit * 1024 * 1024),
        cost_estimate=pl.CostEstimate(flops=flops, bytes_accessed=moved, transcendentals=0),
        name=name,
    )(*operands)


def hub_row_kernel(place_ref, rows_ref, out_ref, block, sem):
    row = place_ref[0, 0]
    first = pl.multiple_of(row // ROWS * ROWS, ROWS)
    copy = pltpu.make_async_copy(rows_ref.at[pl.ds(first, ROWS)], block, sem)
    copy.start()
    copy.wait()
    at = lax.broadcasted_iota(jnp.int32, block.shape, 0) == row - first
    own = jnp.sum(jnp.where(at, block[...].astype(F32), 0.0), axis=0, keepdims=True)
    out_ref[...] = jnp.broadcast_to(split_lanes(own), out_ref.shape)


def hub_row(hub_rows, features, n_z):
    width = features.shape[1]
    return pl.pallas_call(
        hub_row_kernel,
        out_shape=jax.ShapeDtypeStruct((n_z, width // LANES, LANES), F32),
        in_specs=[pl.BlockSpec(memory_space=pltpu.SMEM), pl.BlockSpec(memory_space=pl.ANY)],
        out_specs=pl.BlockSpec(memory_space=pltpu.VMEM),
        scratch_shapes=[pltpu.VMEM((ROWS, width), BF16), pltpu.SemaphoreType.DMA],
        compiler_params=pltpu.CompilerParams(vmem_limit_bytes=60 * 1024 * 1024),
        name="hub_row",
    )(hub_rows, features)


def payload_kernel(along_z, outgoing, out_ref):
    peers, rows, width = out_ref.shape
    hubs = jnp.concatenate([along_z[:, k, :] for k in range(width // LANES)], axis=1)
    hubs = jnp.broadcast_to(hubs[None], (peers, *hubs.shape))
    slots = outgoing[...].astype(F32).reshape(peers, -1, width)
    out_ref[...] = jnp.concatenate([slots, hubs], axis=1).astype(BF16)


def adjacency_kernel(hub_adj, remote_adj, hub_mat, hub_t, remote_mat, remote_t):
    hubs, slots = hub_t.shape[0], remote_t.shape[0]
    n_z = hubs // (CORES * PEERS)

    def source(place):
        at_core, at_peer, at_z = place // (PEERS * n_z), (place // n_z) % PEERS, place % n_z
        return (at_z * CORES + at_core) * PEERS + at_peer

    first = lax.broadcasted_iota(jnp.int32, (hubs, hubs), 0)
    second = lax.broadcasted_iota(jnp.int32, (hubs, hubs), 1)
    hub_rows = hub_adj[...].astype(BF16)
    hub_mat[...] = matmul(hub_rows, (source(second) == first).astype(BF16)).astype(BF16)
    hub_t[...] = back_product((source(first) == second).astype(BF16), hub_rows).astype(BF16)
    remote_rows = remote_adj[...].astype(BF16)
    remote_mat[...] = remote_rows
    same = (first == second)[:slots, :slots].astype(BF16)
    remote_t[...] = back_product(same, remote_rows).astype(BF16)


def middle_kernel(
    hubs, hub_mat, incoming, remote_mat, base, inverse, weight, base_pre, grad, out_ref, pre_ref, mean_ref
):
    peers, width = incoming.shape[0], incoming.shape[2]
    received = incoming[...].astype(F32)[:, : remote_mat.shape[1] // peers]
    received = received.reshape(remote_mat.shape[1], width).astype(BF16)
    total = matmul(hub_mat[...], hubs[...]) + matmul(remote_mat[...], received)
    scale = jnp.concatenate([inverse[...]] * (total.shape[1] // LANES), axis=1)
    mean_feats = ((total + base[...]) * scale).astype(BF16)
    preact = matmul(mean_feats, weight[...]) + base_pre[...]
    low = jnp.minimum(preact, 0.0)
    grown = jnp.exp(low)
    near = low * (1.0 + low * (0.5 + low * (1.0 / 6.0)))
    below = jnp.where(low > -0.02, near, grown - 1.0)
    out_ref[...] = jnp.where(preact > 0, preact, below).astype(BF16)
    grad_pre = (grad[...].astype(F32) * grown).astype(BF16)
    pre_ref[...] = grad_pre
    mean_ref[...] = (back_product(grad_pre, weight[...]) * scale).astype(BF16)


def pack_kernel(remote_t, grad_mean, hub_t, both_means, out_ref):
    peers, rows, width = out_ref.shape
    slots = matmul(remote_t[...], grad_mean[...]).reshape(peers, -1, width)
    nodes = grad_mean.shape[0]
    hubs = matmul(hub_t[0], both_means[:nodes]) + matmul(hub_t[1], both_means[nodes:])
    hubs = hubs.reshape(peers, -1, width)
    out_ref[...] = jnp.concatenate([slots, hubs], axis=1).astype(BF16)


def arrive_kernel(returned, base, out_ref):
    del base
    total = jnp.sum(returned[...].astype(F32), axis=0)
    out_ref[...] = split_lanes(total[total.shape[0] - out_ref.shape[0] :])


def tail_kernel(pick, returned, base, out_ref):
    out_ref[...] = base[...] + matmul(pick[...], returned[...])


def on_device(
    features,
    w_self,
    w_neigh,
    bias_term,
    degree,
    local_adj,
    hub_adj,
    hub_rows,
    remote_adj,
    send_rows,
    send_counts,
    grad_out,
):
    nodes, width = features.shape
    n_z, n_core = lax.axis_size("z"), lax.axis_size("core")
    peers, slots = send_rows.shape[1:]
    hubs = hub_adj.shape[1]
    half = hubs // n_core
    block = slots + n_z
    first_core = lax.axis_index("core") == 0
    rows_f32 = jax.ShapeDtypeStruct((nodes, width), F32)
    rows_b16 = jax.ShapeDtypeStruct((nodes, width), BF16)

    along_z = exchange(hub_row(hub_rows, features, n_z), "z")

    live = jnp.arange(slots, dtype=jnp.int32)[None, :] < send_counts[0][:, None]
    picked = jnp.where(live, send_rows[0], -1)
    at_node = jnp.arange(nodes, dtype=jnp.int32)[:, None]
    pick = (picked.reshape(1, peers * slots) == at_node).astype(BF16)
    outgoing = transposed(pick, features).astype(BF16)
    (payload,) = in_vmem(
        payload_kernel,
        "payload",
        [jax.ShapeDtypeStruct((peers, block, width), BF16)],
        (along_z, outgoing),
        flops=peers * block * width,
    )
    incoming = exchange(payload, DOM)
    same_core = incoming[:, slots:].reshape(half, width)
    all_hubs = lax.all_gather(same_core, "core", axis=0, tiled=True)

    hub_mat, hub_t, remote_mat, remote_t = in_vmem(
        adjacency_kernel,
        "adjacency",
        [jax.ShapeDtypeStruct(shape, BF16) for shape in ((nodes, hubs), (hubs, nodes), (nodes, peers * slots), (peers * slots, nodes))],
        (hub_adj, remote_adj),
        flops=0,
        limit=56,
    )
    chip_t = lax.all_gather(hub_t, "core", axis=0).reshape(n_core, n_core, half, nodes)
    chip_t = jnp.where(first_core, chip_t[:, 0], chip_t[:, 1])
    local_mat = local_adj.astype(BF16)

    base = features.astype(F32) + matmul(local_mat, features)
    base_pre = matmul(features, w_self) + bias_term
    inverse = jnp.broadcast_to(1.0 / (degree.astype(F32)[:, None] + 1.0), (nodes, LANES))
    out_feats, grad_pre, grad_mean = in_vmem(
        middle_kernel,
        "middle",
        [rows_b16] * 3,
        (all_hubs, hub_mat, incoming, remote_mat, base, inverse, w_neigh, base_pre, grad_out),
        flops=2 * nodes * width * (hubs + peers * slots + 2 * width),
    )

    both_means = lax.all_gather(grad_mean, "core", axis=0, tiled=True)
    (payload,) = in_vmem(
        pack_kernel,
        "pack",
        [jax.ShapeDtypeStruct((peers, block, width), BF16)],
        (remote_t, grad_mean, chip_t, both_means),
        flops=2 * 3 * half * nodes * width,
    )
    returned = exchange(payload, DOM)
    grad_base = back_product(grad_pre, w_self) + grad_mean.astype(F32) + transposed(local_mat, grad_mean)
    shape = jax.ShapeDtypeStruct((n_z, width // LANES, LANES), F32)
    (hub_z,) = in_vmem(arrive_kernel, "arrive", [shape], (returned, grad_base), flops=half * width, untouched=1)
    hub_parts = exchange(hub_z, "z")
    hub_grad = jnp.sum(hub_parts, axis=0).reshape(1, width)

    wide = jnp.concatenate([picked, jnp.full((peers, n_z), -1, jnp.int32)], axis=1)
    wide_pick = (wide.reshape(1, peers * block) == at_node).astype(BF16)
    (grad_local,) = in_vmem(
        tail_kernel,
        "tail",
        [rows_f32],
        (wide_pick, returned.reshape(peers * block, width), grad_base),
        flops=2 * nodes * peers * block * width,
    )
    at_hub = at_node == hub_rows[0, 0]
    grad_features = (grad_local + jnp.where(at_hub, hub_grad, 0.0)).astype(BF16)
    return (out_feats, grad_features, hub_grad)


def solution(mesh):
    fine = Mesh(mesh.devices.reshape(8, 2, 4, 8), ALL)
    rows, whole = P(ALL), P()
    return jax.shard_map(
        on_device,
        mesh=fine,
        in_specs=(rows, whole, whole, whole, rows, rows, rows, rows, rows, rows, rows, rows),
        out_specs=(rows, rows, rows),
        check_vma=False,
    )
```

```python
import jax
import jax.numpy as jnp
from jax import lax
from jax.experimental import pallas as pl
from jax.experimental.pallas import tpu as pltpu
from jax.sharding import Mesh
from jax.sharding import PartitionSpec as P

ALL = ("z", "core", "dom")
F32 = jnp.float32
BF16 = jnp.bfloat16
LANES = 128
ROWS = 16
CORES, PEERS = 2, 32


def peer_at(place):
    place = (place + 18) % PEERS
    return place % 4 * 8 + place // 4


PEER_ORDER = [peer_at(k) for k in range(PEERS)]
PEER_PLACE = [PEER_ORDER.index(k) for k in range(PEERS)]
Z_ORDER = [4, 5, 6, 7, 0, 1, 2, 3]


def taken(blocks, places):
    return jnp.concatenate([blocks[k : k + 1] for k in places], axis=0)


def matmul(lhs, rhs):
    return jnp.dot(lhs, rhs, preferred_element_type=F32)


def transposed(matrix, other):
    return lax.dot_general(matrix, other, (((0,), (0,)), ((), ())), preferred_element_type=F32)


def back_product(grads, weight):
    return lax.dot_general(grads, weight, (((1,), (1,)), ((), ())), preferred_element_type=F32)


def exchange(parts, axis, order=None):
    groups = None if order is None else [order]
    return lax.all_to_all(parts, axis, split_axis=0, concat_axis=0, tiled=True, axis_index_groups=groups)


def split_lanes(rows):
    parts = [rows[:, k : k + LANES] for k in range(0, rows.shape[1], LANES)]
    return jnp.stack(parts, axis=1)


def in_vmem(body, name, shapes, operands, flops, limit=8, untouched=0, sent=()):
    spec, anywhere = pl.BlockSpec(memory_space=pltpu.VMEM), pl.BlockSpec(memory_space=pltpu.HBM)
    moved = sum(x.size * x.dtype.itemsize for x in (*operands, *shapes)) if flops else 0
    scratch = [pltpu.VMEM(shapes[k].shape, shapes[k].dtype) for k in sent]
    return pl.pallas_call(
        body,
        out_shape=shapes,
        in_specs=[spec] * (len(operands) - untouched) + [pl.BlockSpec(memory_space=pl.ANY)] * untouched,
        out_specs=[anywhere if k in sent else spec for k in range(len(shapes))],
        scratch_shapes=scratch + [pltpu.SemaphoreType.DMA((2,))] if sent else [],
        compiler_params=pltpu.CompilerParams(vmem_limit_bytes=limit * 1024 * 1024),
        cost_estimate=pl.CostEstimate(flops=flops, bytes_accessed=moved, transcendentals=0),
        name=name,
    )(*operands)


def in_halves(out_ref, held, sem, value):
    half = out_ref.shape[-1] // 2
    copies = []
    for k in range(2):
        columns = slice(k * half, (k + 1) * half)
        held[..., columns] = value(columns)
        copies.append(pltpu.make_async_copy(held.at[..., columns], out_ref.at[..., columns], sem.at[k]))
        copies[k].start()
    for copy in copies:
        copy.wait()


def hub_row_kernel(place_ref, rows_ref, out_ref, block, sem):
    row = place_ref[0, 0]
    first = pl.multiple_of(row // ROWS * ROWS, ROWS)
    copy = pltpu.make_async_copy(rows_ref.at[pl.ds(first, ROWS)], block, sem)
    copy.start()
    copy.wait()
    at = lax.broadcasted_iota(jnp.int32, block.shape, 0) == row - first
    own = jnp.sum(jnp.where(at, block[...].astype(F32), 0.0), axis=0, keepdims=True)
    out_ref[...] = jnp.broadcast_to(split_lanes(own), out_ref.shape)


def hub_row(hub_rows, features, n_z):
    width = features.shape[1]
    return pl.pallas_call(
        hub_row_kernel,
        out_shape=jax.ShapeDtypeStruct((n_z, width // LANES, LANES), F32),
        in_specs=[pl.BlockSpec(memory_space=pltpu.SMEM), pl.BlockSpec(memory_space=pl.ANY)],
        out_specs=pl.BlockSpec(memory_space=pltpu.VMEM),
        scratch_shapes=[pltpu.VMEM((ROWS, width), BF16), pltpu.SemaphoreType.DMA],
        compiler_params=pltpu.CompilerParams(vmem_limit_bytes=60 * 1024 * 1024),
        name="hub_row",
    )(hub_rows, features)


def payload_kernel(along_z, outgoing, out_ref, held, sem):
    peers = out_ref.shape[0]

    def value(columns):
        parts = [along_z[:, k // LANES, :] for k in range(columns.start, columns.stop, LANES)]
        hubs = jnp.concatenate(parts, axis=1)
        hubs = jnp.broadcast_to(hubs[None], (peers, *hubs.shape))
        slots = outgoing[:, columns].astype(F32).reshape(peers, -1, hubs.shape[2])
        return jnp.concatenate([taken(slots, PEER_ORDER), hubs], axis=1).astype(BF16)

    in_halves(out_ref, held, sem, value)


def adjacency_kernel(hub_adj, remote_adj, hub_mat, hub_t, remote_mat, remote_t):
    hubs, slots = hub_t.shape[0], remote_t.shape[0]
    n_z = hubs // (CORES * PEERS)

    def source(place):
        at_core, at_peer, at_z = place // (PEERS * n_z), (place // n_z) % PEERS, place % n_z
        return (at_z * CORES + at_core) * PEERS + peer_at(at_peer)

    first = lax.broadcasted_iota(jnp.int32, (hubs, hubs), 0)
    second = lax.broadcasted_iota(jnp.int32, (hubs, hubs), 1)
    hub_rows = hub_adj[...].astype(BF16)
    hub_mat[...] = matmul(hub_rows, (source(second) == first).astype(BF16)).astype(BF16)
    hub_t[...] = back_product((source(first) == second).astype(BF16), hub_rows).astype(BF16)
    remote_rows = remote_adj[...].astype(BF16)
    remote_mat[...] = remote_rows
    same = (first == second)[:slots, :slots].astype(BF16)
    remote_t[...] = back_product(same, remote_rows).astype(BF16)


def middle_kernel(
    hubs, hub_mat, incoming, remote_mat, base, inverse, weight, base_pre, grad, out_ref, pre_ref, mean_ref, out, pre, sem
):
    peers, width = incoming.shape[0], incoming.shape[2]
    received = incoming[...].astype(F32)[:, : remote_mat.shape[1] // peers]
    received = taken(received, PEER_PLACE).reshape(remote_mat.shape[1], width).astype(BF16)
    total = matmul(hub_mat[...], hubs[...]) + matmul(remote_mat[...], received)
    scale = jnp.concatenate([inverse[...]] * (total.shape[1] // LANES), axis=1)
    mean_feats = ((total + base[...]) * scale).astype(BF16)
    preact = matmul(mean_feats, weight[...]) + base_pre[...]
    low = jnp.minimum(preact, 0.0)
    grown = jnp.exp(low)
    near = low * (1.0 + low * (0.5 + low * (1.0 / 6.0)))
    below = jnp.where(low > -0.02, near, grown - 1.0)
    out[...] = jnp.where(preact > 0, preact, below).astype(BF16)
    grad_pre = (grad[...].astype(F32) * grown).astype(BF16)
    pre[...] = grad_pre
    copies = [pltpu.make_async_copy(*pair, sem.at[k]) for k, pair in enumerate(((out, out_ref), (pre, pre_ref)))]
    for copy in copies:
        copy.start()
    mean_ref[...] = (back_product(grad_pre, weight[...]) * scale).astype(BF16)
    for copy in copies:
        copy.wait()


def pack_kernel(remote_t, grad_mean, hub_t, both_means, grad_pre, out_ref, held, sem):
    del grad_pre
    peers, nodes = out_ref.shape[0], grad_mean.shape[0]

    def value(columns):
        slots = matmul(remote_t[...], grad_mean[:, columns])
        hubs = matmul(hub_t[0], both_means[:nodes, columns]) + matmul(hub_t[1], both_means[nodes:, columns])
        slots, hubs = (x.reshape(peers, -1, x.shape[1]) for x in (slots, hubs))
        return jnp.concatenate([taken(slots, PEER_ORDER), hubs], axis=1).astype(BF16)

    in_halves(out_ref, held, sem, value)


def arrive_kernel(returned, base, out_ref):
    del base
    total = jnp.sum(returned[...].astype(F32), axis=0)
    out_ref[...] = taken(split_lanes(total[total.shape[0] - out_ref.shape[0] :]), Z_ORDER)


def tail_kernel(pick, returned, base, at_hub, out_ref):
    del at_hub
    blocks = taken(returned[...], PEER_PLACE)
    out_ref[...] = base[...] + matmul(pick[...], blocks.reshape(-1, blocks.shape[2]))


def last_kernel(grad_local, at_hub, parts, out_ref, hub_ref, held, held_hub, sem):
    total = jnp.sum(parts[...], axis=0)
    hub = jnp.concatenate([total[k : k + 1] for k in range(total.shape[0])], axis=1)
    held_hub[...] = hub
    here = jnp.concatenate([at_hub[...]] * total.shape[0], axis=1) > 0
    held[...] = (grad_local[...] + jnp.where(here, hub, 0.0)).astype(BF16)
    copies = [pltpu.make_async_copy(*pair, sem.at[k]) for k, pair in enumerate(((held, out_ref), (held_hub, hub_ref)))]
    for copy in copies:
        copy.start()
    for copy in copies:
        copy.wait()


def on_device(
    features,
    w_self,
    w_neigh,
    bias_term,
    degree,
    local_adj,
    hub_adj,
    hub_rows,
    remote_adj,
    send_rows,
    send_counts,
    grad_out,
):
    nodes, width = features.shape
    n_z, n_core = lax.axis_size("z"), lax.axis_size("core")
    peers, slots = send_rows.shape[1:]
    hubs = hub_adj.shape[1]
    half = hubs // n_core
    block = slots + n_z
    first_core = lax.axis_index("core") == 0
    rows_f32 = jax.ShapeDtypeStruct((nodes, width), F32)
    rows_b16 = jax.ShapeDtypeStruct((nodes, width), BF16)

    along_z = exchange(hub_row(hub_rows, features, n_z), "z")

    live = jnp.arange(slots, dtype=jnp.int32)[None, :] < send_counts[0][:, None]
    picked = jnp.where(live, send_rows[0], -1)
    at_node = jnp.arange(nodes, dtype=jnp.int32)[:, None]
    pick = (picked.reshape(1, peers * slots) == at_node).astype(BF16)
    outgoing = transposed(pick, features).astype(BF16)
    (payload,) = in_vmem(
        payload_kernel,
        "payload",
        [jax.ShapeDtypeStruct((peers, block, width), BF16)],
        (along_z, outgoing),
        flops=peers * block * width,
        sent=(0,),
    )
    incoming = exchange(payload, "dom", PEER_ORDER)
    same_core = incoming[:, slots:].reshape(half, width)
    all_hubs = lax.all_gather(same_core, "core", axis=0, tiled=True)

    hub_mat, hub_t, remote_mat, remote_t = in_vmem(
        adjacency_kernel,
        "adjacency",
        [jax.ShapeDtypeStruct(shape, BF16) for shape in ((nodes, hubs), (hubs, nodes), (nodes, peers * slots), (peers * slots, nodes))],
        (hub_adj, remote_adj),
        flops=0,
        limit=56,
    )
    chip_t = lax.all_gather(hub_t, "core", axis=0).reshape(n_core, n_core, half, nodes)
    chip_t = jnp.where(first_core, chip_t[:, 0], chip_t[:, 1])
    local_mat = local_adj.astype(BF16)

    base = features.astype(F32) + matmul(local_mat, features)
    base_pre = matmul(features, w_self) + bias_term
    inverse = jnp.broadcast_to(1.0 / (degree.astype(F32)[:, None] + 1.0), (nodes, LANES))
    out_feats, grad_pre, grad_mean = in_vmem(
        middle_kernel,
        "middle",
        [rows_b16] * 3,
        (all_hubs, hub_mat, incoming, remote_mat, base, inverse, w_neigh, base_pre, grad_out),
        flops=2 * nodes * width * (hubs + peers * slots + 2 * width),
        sent=(0, 1),
    )

    both_means = lax.all_gather(grad_mean, "core", axis=0, tiled=True)
    (payload,) = in_vmem(
        pack_kernel,
        "pack",
        [jax.ShapeDtypeStruct((peers, block, width), BF16)],
        (remote_t, grad_mean, chip_t, both_means, grad_pre),
        flops=2 * 3 * half * nodes * width,
        untouched=1,
        sent=(0,),
    )
    returned = exchange(payload, "dom", PEER_ORDER)
    grad_base = back_product(grad_pre, w_self) + grad_mean.astype(F32) + transposed(local_mat, grad_mean)
    shape = jax.ShapeDtypeStruct((n_z, width // LANES, LANES), F32)
    at_hub = jnp.broadcast_to((at_node == hub_rows[0, 0]).astype(F32), (nodes, LANES))
    (hub_z,) = in_vmem(arrive_kernel, "arrive", [shape], (returned, grad_base), flops=half * width, untouched=1)
    hub_parts = exchange(hub_z, "z", Z_ORDER)

    wide = jnp.concatenate([picked, jnp.full((peers, n_z), -1, jnp.int32)], axis=1)
    wide_pick = (wide.reshape(1, peers * block) == at_node).astype(BF16)
    (grad_local,) = in_vmem(
        tail_kernel,
        "tail",
        [rows_f32],
        (wide_pick, returned, grad_base, at_hub),
        flops=2 * nodes * peers * block * width,
        untouched=1,
    )
    grad_features, hub_grad = in_vmem(
        last_kernel,
        "last",
        [rows_b16, jax.ShapeDtypeStruct((1, width), F32)],
        (grad_local, at_hub, hub_parts),
        flops=nodes * width,
        sent=(0, 1),
    )
    return (out_feats, grad_features, hub_grad)


def solution(mesh):
    fine = Mesh(mesh.devices.reshape(8, CORES, PEERS), ALL)
    rows, whole = P(ALL), P()
    return jax.shard_map(
        on_device,
        mesh=fine,
        in_specs=(rows, whole, whole, whole, rows, rows, rows, rows, rows, rows, rows, rows),
        out_specs=(rows, rows, rows),
        check_vma=False,
    )
```

```python
import jax
import jax.numpy as jnp
from jax import lax
from jax.experimental import pallas as pl
from jax.experimental.pallas import tpu as pltpu
from jax.sharding import Mesh
from jax.sharding import PartitionSpec as P

ALL = ("z", "core", "dom")
F32 = jnp.float32
BF16 = jnp.bfloat16
LANES = 128
ROWS = 16
CORES, PEERS = 2, 32


def peer_at(place):
    place = (place + 18) & (PEERS - 1)
    return ((place & 3) << 3) | (place >> 2)


PEER_ORDER = [peer_at(k) for k in range(PEERS)]
PEER_PLACE = [PEER_ORDER.index(k) for k in range(PEERS)]
Z_ORDER = [4, 5, 6, 7, 0, 1, 2, 3]


def taken(blocks, places):
    return jnp.concatenate([blocks[k : k + 1] for k in places], axis=0)


def matmul(lhs, rhs):
    return jnp.dot(lhs, rhs, preferred_element_type=F32)


def transposed(matrix, other):
    return lax.dot_general(matrix, other, (((0,), (0,)), ((), ())), preferred_element_type=F32)


def back_product(grads, weight):
    return lax.dot_general(grads, weight, (((1,), (1,)), ((), ())), preferred_element_type=F32)


def exchange(parts, axis, order=None):
    groups = None if order is None else [order]
    return lax.all_to_all(parts, axis, split_axis=0, concat_axis=0, tiled=True, axis_index_groups=groups)


def split_lanes(rows):
    parts = [rows[:, k : k + LANES] for k in range(0, rows.shape[1], LANES)]
    return jnp.stack(parts, axis=1)


def in_vmem(body, name, shapes, operands, flops, limit=8, untouched=0, sent=()):
    spec, anywhere = pl.BlockSpec(memory_space=pltpu.VMEM), pl.BlockSpec(memory_space=pltpu.HBM)
    moved = sum(x.size * x.dtype.itemsize for x in (*operands, *shapes)) if flops else 0
    scratch = [pltpu.VMEM(shapes[k].shape, shapes[k].dtype) for k in sent]
    return pl.pallas_call(
        body,
        out_shape=shapes,
        in_specs=[spec] * (len(operands) - untouched) + [pl.BlockSpec(memory_space=pl.ANY)] * untouched,
        out_specs=[anywhere if k in sent else spec for k in range(len(shapes))],
        scratch_shapes=scratch + [pltpu.SemaphoreType.DMA((2,))] if sent else [],
        compiler_params=pltpu.CompilerParams(vmem_limit_bytes=limit * 1024 * 1024),
        cost_estimate=pl.CostEstimate(flops=flops, bytes_accessed=moved, transcendentals=0),
        name=name,
    )(*operands)


def in_halves(out_ref, held, sem, value):
    half = out_ref.shape[-1] // 2
    copies = []
    for k in range(2):
        columns = slice(k * half, (k + 1) * half)
        held[..., columns] = value(columns)
        copies.append(pltpu.make_async_copy(held.at[..., columns], out_ref.at[..., columns], sem.at[k]))
        copies[k].start()
    for copy in copies:
        copy.wait()


def hub_row_kernel(place_ref, rows_ref, out_ref, block, sem):
    row = place_ref[0, 0]
    first = pl.multiple_of(row // ROWS * ROWS, ROWS)
    copy = pltpu.make_async_copy(rows_ref.at[pl.ds(first, ROWS)], block, sem)
    copy.start()
    copy.wait()
    at = lax.broadcasted_iota(jnp.int32, block.shape, 0) == row - first
    own = jnp.sum(jnp.where(at, block[...].astype(F32), 0.0), axis=0, keepdims=True)
    out_ref[...] = jnp.broadcast_to(split_lanes(own), out_ref.shape)


def hub_row(hub_rows, features, n_z):
    width = features.shape[1]
    return pl.pallas_call(
        hub_row_kernel,
        out_shape=jax.ShapeDtypeStruct((n_z, width // LANES, LANES), F32),
        in_specs=[pl.BlockSpec(memory_space=pltpu.SMEM), pl.BlockSpec(memory_space=pl.ANY)],
        out_specs=pl.BlockSpec(memory_space=pltpu.VMEM),
        scratch_shapes=[pltpu.VMEM((ROWS, width), BF16), pltpu.SemaphoreType.DMA],
        compiler_params=pltpu.CompilerParams(vmem_limit_bytes=60 * 1024 * 1024),
        name="hub_row",
    )(hub_rows, features)


def payload_kernel(along_z, outgoing, out_ref, held, sem):
    peers = out_ref.shape[0]

    def value(columns):
        parts = [along_z[:, k // LANES, :] for k in range(columns.start, columns.stop, LANES)]
        hubs = jnp.concatenate(parts, axis=1)
        hubs = jnp.broadcast_to(hubs[None], (peers, *hubs.shape))
        slots = outgoing[:, columns].astype(F32).reshape(peers, -1, hubs.shape[2])
        return jnp.concatenate([taken(slots, PEER_ORDER), hubs], axis=1).astype(BF16)

    in_halves(out_ref, held, sem, value)


def adjacency_kernel(hub_adj, remote_adj, hub_mat, hub_t, remote_mat, remote_t):
    hubs, slots = hub_t.shape[0], remote_t.shape[0]
    n_z = hubs // (CORES * PEERS)
    shift = n_z.bit_length() - 1

    def source(place):
        at_core, at_peer, at_z = place >> shift + 5, (place >> shift) & (PEERS - 1), (place + Z_ORDER[0]) & (n_z - 1)
        return (at_z * CORES + at_core) * PEERS + peer_at(at_peer)

    column = lax.broadcasted_iota(jnp.int32, (hubs, 1), 0)
    row = lax.broadcasted_iota(jnp.int32, (1, hubs), 1)
    hub_rows = hub_adj[...].astype(BF16)
    hub_mat[...] = matmul(hub_rows, (source(row) == column).astype(BF16)).astype(BF16)
    hub_t[...] = back_product((source(column) == row).astype(BF16), hub_rows).astype(BF16)
    remote_rows = remote_adj[...].astype(BF16)
    remote_mat[...] = remote_rows
    same = (column[:slots] == row[:, :slots]).astype(BF16)
    remote_t[...] = back_product(same, remote_rows).astype(BF16)


def middle_kernel(
    hubs, hub_mat, incoming, remote_mat, base, inverse, weight, base_pre, grad, out_ref, pre_ref, mean_ref, out, pre, sem
):
    peers, width = incoming.shape[0], incoming.shape[2]
    received = incoming[...].astype(F32)[:, : remote_mat.shape[1] // peers]
    received = taken(received, PEER_PLACE).reshape(remote_mat.shape[1], width).astype(BF16)
    total = matmul(hub_mat[...], hubs[...]) + matmul(remote_mat[...], received)
    scale = jnp.concatenate([inverse[...]] * (total.shape[1] // LANES), axis=1)
    mean_feats = ((total + base[...]) * scale).astype(BF16)
    preact = matmul(mean_feats, weight[...]) + base_pre[...]
    low = jnp.minimum(preact, 0.0)
    grown = jnp.exp(low)
    near = low * (1.0 + low * (0.5 + low * (1.0 / 6.0)))
    below = jnp.where(low > -0.02, near, grown - 1.0)
    out[...] = jnp.where(preact > 0, preact, below).astype(BF16)
    grad_pre = (grad[...].astype(F32) * grown).astype(BF16)
    pre[...] = grad_pre
    copies = [pltpu.make_async_copy(*pair, sem.at[k]) for k, pair in enumerate(((out, out_ref), (pre, pre_ref)))]
    for copy in copies:
        copy.start()
    mean_ref[...] = (back_product(grad_pre, weight[...]) * scale).astype(BF16)
    for copy in copies:
        copy.wait()


def pack_kernel(remote_t, grad_mean, hub_t, both_means, grad_pre, out_ref, held, sem):
    del grad_pre
    peers, nodes = out_ref.shape[0], grad_mean.shape[0]

    def value(columns):
        slots = matmul(remote_t[...], grad_mean[:, columns])
        hubs = matmul(hub_t[0], both_means[:nodes, columns]) + matmul(hub_t[1], both_means[nodes:, columns])
        slots, hubs = (x.reshape(peers, -1, x.shape[1]) for x in (slots, hubs))
        return jnp.concatenate([taken(slots, PEER_ORDER), hubs], axis=1).astype(BF16)

    in_halves(out_ref, held, sem, value)


def arrive_kernel(returned, base, out_ref):
    del base
    total = jnp.sum(returned[...].astype(F32), axis=0)
    out_ref[...] = split_lanes(total[total.shape[0] - out_ref.shape[0] :])


def tail_kernel(pick, returned, base, at_hub, out_ref):
    del at_hub
    blocks = taken(returned[...], PEER_PLACE)
    out_ref[...] = base[...] + matmul(pick[...], blocks.reshape(-1, blocks.shape[2]))


def last_kernel(grad_local, at_hub, parts, out_ref, hub_ref, held, held_hub, sem):
    total = jnp.sum(parts[...], axis=0)
    hub = jnp.concatenate([total[k : k + 1] for k in range(total.shape[0])], axis=1)
    held_hub[...] = hub
    here = jnp.concatenate([at_hub[...]] * total.shape[0], axis=1) > 0
    held[...] = (grad_local[...] + jnp.where(here, hub, 0.0)).astype(BF16)
    copies = [pltpu.make_async_copy(*pair, sem.at[k]) for k, pair in enumerate(((held, out_ref), (held_hub, hub_ref)))]
    for copy in copies:
        copy.start()
    for copy in copies:
        copy.wait()


def on_device(
    features,
    w_self,
    w_neigh,
    bias_term,
    degree,
    local_adj,
    hub_adj,
    hub_rows,
    remote_adj,
    send_rows,
    send_counts,
    grad_out,
):
    nodes, width = features.shape
    n_z, n_core = lax.axis_size("z"), lax.axis_size("core")
    peers, slots = send_rows.shape[1:]
    hubs = hub_adj.shape[1]
    half = hubs // n_core
    block = slots + n_z
    first_core = lax.axis_index("core") == 0
    rows_f32 = jax.ShapeDtypeStruct((nodes, width), F32)
    rows_b16 = jax.ShapeDtypeStruct((nodes, width), BF16)

    along_z = exchange(hub_row(hub_rows, features, n_z), "z", Z_ORDER)

    live = jnp.arange(slots, dtype=jnp.int32)[None, :] < send_counts[0][:, None]
    picked = jnp.where(live, send_rows[0], -1)
    at_node = jnp.arange(nodes, dtype=jnp.int32)[:, None]
    pick = (picked.reshape(1, peers * slots) == at_node).astype(BF16)
    outgoing = transposed(pick, features).astype(BF16)
    (payload,) = in_vmem(
        payload_kernel,
        "payload",
        [jax.ShapeDtypeStruct((peers, block, width), BF16)],
        (along_z, outgoing),
        flops=peers * block * width,
        sent=(0,),
    )
    incoming = exchange(payload, "dom", PEER_ORDER)
    same_core = incoming[:, slots:].reshape(half, width)
    all_hubs = lax.all_gather(same_core, "core", axis=0, tiled=True)

    hub_mat, hub_t, remote_mat, remote_t = in_vmem(
        adjacency_kernel,
        "adjacency",
        [jax.ShapeDtypeStruct(shape, BF16) for shape in ((nodes, hubs), (hubs, nodes), (nodes, peers * slots), (peers * slots, nodes))],
        (hub_adj, remote_adj),
        flops=0,
        limit=56,
    )
    chip_t = lax.all_gather(hub_t, "core", axis=0).reshape(n_core, n_core, half, nodes)
    chip_t = jnp.where(first_core, chip_t[:, 0], chip_t[:, 1])
    local_mat = local_adj.astype(BF16)

    base = features.astype(F32) + matmul(local_mat, features)
    base_pre = matmul(features, w_self) + bias_term
    inverse = jnp.broadcast_to(1.0 / (degree.astype(F32)[:, None] + 1.0), (nodes, LANES))
    out_feats, grad_pre, grad_mean = in_vmem(
        middle_kernel,
        "middle",
        [rows_b16] * 3,
        (all_hubs, hub_mat, incoming, remote_mat, base, inverse, w_neigh, base_pre, grad_out),
        flops=2 * nodes * width * (hubs + peers * slots + 2 * width),
        sent=(0, 1),
    )

    both_means = lax.all_gather(grad_mean, "core", axis=0, tiled=True)
    (payload,) = in_vmem(
        pack_kernel,
        "pack",
        [jax.ShapeDtypeStruct((peers, block, width), BF16)],
        (remote_t, grad_mean, chip_t, both_means, grad_pre),
        flops=2 * 3 * half * nodes * width,
        untouched=1,
        sent=(0,),
    )
    returned = exchange(payload, "dom", PEER_ORDER)
    grad_base = back_product(grad_pre, w_self) + grad_mean.astype(F32) + transposed(local_mat, grad_mean)
    shape = jax.ShapeDtypeStruct((n_z, width // LANES, LANES), F32)
    at_hub = jnp.broadcast_to((at_node == hub_rows[0, 0]).astype(F32), (nodes, LANES))
    (hub_z,) = in_vmem(arrive_kernel, "arrive", [shape], (returned, grad_base), flops=half * width, untouched=1)
    hub_parts = exchange(hub_z, "z", Z_ORDER)

    wide = jnp.concatenate([picked, jnp.full((peers, n_z), -1, jnp.int32)], axis=1)
    wide_pick = (wide.reshape(1, peers * block) == at_node).astype(BF16)
    (grad_local,) = in_vmem(
        tail_kernel,
        "tail",
        [rows_f32],
        (wide_pick, returned, grad_base, at_hub),
        flops=2 * nodes * peers * block * width,
        untouched=1,
    )
    grad_features, hub_grad = in_vmem(
        last_kernel,
        "last",
        [rows_b16, jax.ShapeDtypeStruct((1, width), F32)],
        (grad_local, at_hub, hub_parts),
        flops=nodes * width,
        sent=(0, 1),
    )
    return (out_feats, grad_features, hub_grad)


def solution(mesh):
    fine = Mesh(mesh.devices.reshape(8, CORES, PEERS), ALL)
    rows, whole = P(ALL), P()
    return jax.shard_map(
        on_device,
        mesh=fine,
        in_specs=(rows, whole, whole, whole, rows, rows, rows, rows, rows, rows, rows, rows),
        out_specs=(rows, rows, rows),
        check_vma=False,
    )
```

```python
import jax
import jax.numpy as jnp
from jax import lax
from jax.experimental import pallas as pl
from jax.experimental.pallas import tpu as pltpu
from jax.sharding import Mesh
from jax.sharding import PartitionSpec as P

ALL = ("z", "core", "dom")
F32 = jnp.float32
BF16 = jnp.bfloat16
LANES = 128
ROWS = 16
CORES, PEERS = 2, 32


def peer_at(place):
    place = (place + 18) & (PEERS - 1)
    return ((place & 3) << 3) | (place >> 2)


PEER_ORDER = [peer_at(k) for k in range(PEERS)]
PEER_PLACE = [PEER_ORDER.index(k) for k in range(PEERS)]
Z_ORDER = [4, 5, 6, 7, 0, 1, 2, 3]


def taken(blocks, places):
    return jnp.concatenate([blocks[k : k + 1] for k in places], axis=0)


def matmul(lhs, rhs):
    return jnp.dot(lhs, rhs, preferred_element_type=F32)


def transposed(matrix, other):
    return lax.dot_general(matrix, other, (((0,), (0,)), ((), ())), preferred_element_type=F32)


def back_product(grads, weight):
    return lax.dot_general(grads, weight, (((1,), (1,)), ((), ())), preferred_element_type=F32)


def exchange(parts, axis, order=None):
    groups = None if order is None else [order]
    return lax.all_to_all(parts, axis, split_axis=0, concat_axis=0, tiled=True, axis_index_groups=groups)


def split_lanes(rows):
    parts = [rows[:, k : k + LANES] for k in range(0, rows.shape[1], LANES)]
    return jnp.stack(parts, axis=1)


def in_vmem(body, name, shapes, operands, flops, limit=8, untouched=0, sent=()):
    spec, anywhere = pl.BlockSpec(memory_space=pltpu.VMEM), pl.BlockSpec(memory_space=pltpu.HBM)
    moved = sum(x.size * x.dtype.itemsize for x in (*operands, *shapes)) if flops else 0
    scratch = [pltpu.VMEM(shapes[k].shape, shapes[k].dtype) for k in sent]
    return pl.pallas_call(
        body,
        out_shape=shapes,
        in_specs=[spec] * (len(operands) - untouched) + [pl.BlockSpec(memory_space=pl.ANY)] * untouched,
        out_specs=[anywhere if k in sent else spec for k in range(len(shapes))],
        scratch_shapes=scratch + [pltpu.SemaphoreType.DMA((2,))] if sent else [],
        compiler_params=pltpu.CompilerParams(vmem_limit_bytes=limit * 1024 * 1024),
        cost_estimate=pl.CostEstimate(flops=flops, bytes_accessed=moved, transcendentals=0),
        name=name,
    )(*operands)


def in_halves(out_ref, held, sem, value):
    half = out_ref.shape[-1] // 2
    copies = []
    for k in range(2):
        columns = slice(k * half, (k + 1) * half)
        held[..., columns] = value(columns)
        copies.append(pltpu.make_async_copy(held.at[..., columns], out_ref.at[..., columns], sem.at[k]))
        copies[k].start()
    for copy in copies:
        copy.wait()


def hub_row_kernel(place_ref, rows_ref, out_ref, block, sem):
    row = place_ref[0, 0]
    first = pl.multiple_of(row // ROWS * ROWS, ROWS)
    copy = pltpu.make_async_copy(rows_ref.at[pl.ds(first, ROWS)], block, sem)
    copy.start()
    copy.wait()
    at = lax.broadcasted_iota(jnp.int32, block.shape, 0) == row - first
    own = jnp.sum(jnp.where(at, block[...].astype(F32), 0.0), axis=0, keepdims=True)
    out_ref[...] = jnp.broadcast_to(split_lanes(own), out_ref.shape)


def hub_row(hub_rows, features, n_z):
    width = features.shape[1]
    return pl.pallas_call(
        hub_row_kernel,
        out_shape=jax.ShapeDtypeStruct((n_z, width // LANES, LANES), F32),
        in_specs=[pl.BlockSpec(memory_space=pltpu.SMEM), pl.BlockSpec(memory_space=pl.ANY)],
        out_specs=pl.BlockSpec(memory_space=pltpu.VMEM),
        scratch_shapes=[pltpu.VMEM((ROWS, width), BF16), pltpu.SemaphoreType.DMA],
        compiler_params=pltpu.CompilerParams(vmem_limit_bytes=60 * 1024 * 1024),
        name="hub_row",
    )(hub_rows, features)


def payload_kernel(along_z, outgoing, base, base_pre, out_ref, held, sem):
    del base, base_pre
    peers = out_ref.shape[0]

    def value(columns):
        parts = [along_z[:, k // LANES, :] for k in range(columns.start, columns.stop, LANES)]
        hubs = jnp.concatenate(parts, axis=1)
        hubs = jnp.broadcast_to(hubs[None], (peers, *hubs.shape))
        slots = outgoing[:, columns].astype(F32).reshape(peers, -1, hubs.shape[2])
        return jnp.concatenate([taken(slots, PEER_ORDER), hubs], axis=1).astype(BF16)

    in_halves(out_ref, held, sem, value)


def adjacency_kernel(hub_adj, remote_adj, hub_mat, hub_t, remote_mat, remote_t):
    hubs, slots = hub_t.shape[0], remote_t.shape[0]
    n_z = hubs // (CORES * PEERS)
    shift = n_z.bit_length() - 1

    def source(place):
        at_core, at_peer, at_z = place >> shift + 5, (place >> shift) & (PEERS - 1), place & (n_z - 1)
        return (at_z * CORES + at_core) * PEERS + peer_at(at_peer)

    column = lax.broadcasted_iota(jnp.int32, (hubs, 1), 0)
    row = lax.broadcasted_iota(jnp.int32, (1, hubs), 1)
    hub_rows = hub_adj[...].astype(BF16)
    hub_mat[...] = matmul(hub_rows, (source(row) == column).astype(BF16)).astype(BF16)
    hub_t[...] = back_product((source(column) == row).astype(BF16), hub_rows).astype(BF16)
    remote_rows = remote_adj[...].astype(BF16)
    remote_mat[...] = remote_rows
    same = (column[:slots] == row[:, :slots]).astype(BF16)
    remote_t[...] = back_product(same, remote_rows).astype(BF16)


def middle_kernel(
    hubs, hub_mat, incoming, remote_mat, base, inverse, weight, base_pre, grad, out_ref, pre_ref, mean_ref, out, pre, sem
):
    peers, width = incoming.shape[0], incoming.shape[2]
    received = incoming[...].astype(F32)[:, : remote_mat.shape[1] // peers]
    received = taken(received, PEER_PLACE).reshape(remote_mat.shape[1], width).astype(BF16)
    total = matmul(hub_mat[...], hubs[...]) + matmul(remote_mat[...], received)
    scale = jnp.concatenate([inverse[...]] * (total.shape[1] // LANES), axis=1)
    mean_feats = ((total + base[...]) * scale).astype(BF16)
    preact = matmul(mean_feats, weight[...]) + base_pre[...]
    low = jnp.minimum(preact, 0.0)
    grown = jnp.exp(low)
    near = low * (1.0 + low * (0.5 + low * (1.0 / 6.0)))
    below = jnp.where(low > -0.02, near, grown - 1.0)
    out[...] = jnp.where(preact > 0, preact, below).astype(BF16)
    grad_pre = (grad[...].astype(F32) * grown).astype(BF16)
    pre[...] = grad_pre
    copies = [pltpu.make_async_copy(*pair, sem.at[k]) for k, pair in enumerate(((out, out_ref), (pre, pre_ref)))]
    for copy in copies:
        copy.start()
    mean_ref[...] = (back_product(grad_pre, weight[...]) * scale).astype(BF16)
    for copy in copies:
        copy.wait()


def pack_kernel(remote_t, grad_mean, hub_t, both_means, grad_pre, out_ref, held, sem):
    del grad_pre
    peers, nodes = out_ref.shape[0], grad_mean.shape[0]

    def value(columns):
        slots = matmul(remote_t[...], grad_mean[:, columns])
        hubs = matmul(hub_t[0], both_means[:nodes, columns]) + matmul(hub_t[1], both_means[nodes:, columns])
        slots, hubs = (x.reshape(peers, -1, x.shape[1]) for x in (slots, hubs))
        return jnp.concatenate([taken(slots, PEER_ORDER), hubs], axis=1).astype(BF16)

    in_halves(out_ref, held, sem, value)


def arrive_kernel(returned, base, out_ref):
    del base
    total = jnp.sum(returned[...].astype(F32), axis=0)
    out_ref[...] = taken(split_lanes(total[total.shape[0] - out_ref.shape[0] :]), Z_ORDER)


def tail_kernel(pick, returned, base, at_hub, out_ref):
    del at_hub
    blocks = taken(returned[...], PEER_PLACE)
    out_ref[...] = base[...] + matmul(pick[...], blocks.reshape(-1, blocks.shape[2]))


def last_kernel(grad_local, at_hub, parts, out_ref, hub_ref, held, held_hub, sem):
    total = jnp.sum(parts[...], axis=0)
    hub = jnp.concatenate([total[k : k + 1] for k in range(total.shape[0])], axis=1)
    held_hub[...] = hub
    here = jnp.concatenate([at_hub[...]] * total.shape[0], axis=1) > 0
    held[...] = (grad_local[...] + jnp.where(here, hub, 0.0)).astype(BF16)
    copies = [pltpu.make_async_copy(*pair, sem.at[k]) for k, pair in enumerate(((held, out_ref), (held_hub, hub_ref)))]
    for copy in copies:
        copy.start()
    for copy in copies:
        copy.wait()


def on_device(
    features,
    w_self,
    w_neigh,
    bias_term,
    degree,
    local_adj,
    hub_adj,
    hub_rows,
    remote_adj,
    send_rows,
    send_counts,
    grad_out,
):
    nodes, width = features.shape
    n_z, n_core = lax.axis_size("z"), lax.axis_size("core")
    peers, slots = send_rows.shape[1:]
    hubs = hub_adj.shape[1]
    half = hubs // n_core
    block = slots + n_z
    first_core = lax.axis_index("core") == 0
    rows_f32 = jax.ShapeDtypeStruct((nodes, width), F32)
    rows_b16 = jax.ShapeDtypeStruct((nodes, width), BF16)

    along_z = exchange(hub_row(hub_rows, features, n_z), "z")

    live = jnp.arange(slots, dtype=jnp.int32)[None, :] < send_counts[0][:, None]
    picked = jnp.where(live, send_rows[0], -1)
    at_node = jnp.arange(nodes, dtype=jnp.int32)[:, None]
    pick = (picked.reshape(1, peers * slots) == at_node).astype(BF16)
    outgoing = transposed(pick, features).astype(BF16)
    local_mat = local_adj.astype(BF16)
    base = features.astype(F32) + matmul(local_mat, features)
    base_pre = matmul(features, w_self) + bias_term
    (payload,) = in_vmem(
        payload_kernel,
        "payload",
        [jax.ShapeDtypeStruct((peers, block, width), BF16)],
        (along_z, outgoing, base, base_pre),
        flops=peers * block * width,
        untouched=2,
        sent=(0,),
    )
    incoming = exchange(payload, "dom", PEER_ORDER)
    same_core = incoming[:, slots:].reshape(half, width)
    all_hubs = lax.all_gather(same_core, "core", axis=0, tiled=True)

    hub_mat, hub_t, remote_mat, remote_t = in_vmem(
        adjacency_kernel,
        "adjacency",
        [jax.ShapeDtypeStruct(shape, BF16) for shape in ((nodes, hubs), (hubs, nodes), (nodes, peers * slots), (peers * slots, nodes))],
        (hub_adj, remote_adj),
        flops=0,
        limit=56,
    )
    chip_t = lax.all_gather(hub_t, "core", axis=0).reshape(n_core, n_core, half, nodes)
    chip_t = jnp.where(first_core, chip_t[:, 0], chip_t[:, 1])

    inverse = jnp.broadcast_to(1.0 / (degree.astype(F32)[:, None] + 1.0), (nodes, LANES))
    out_feats, grad_pre, grad_mean = in_vmem(
        middle_kernel,
        "middle",
        [rows_b16] * 3,
        (all_hubs, hub_mat, incoming, remote_mat, base, inverse, w_neigh, base_pre, grad_out),
        flops=2 * nodes * width * (hubs + peers * slots + 2 * width),
        sent=(0, 1),
    )

    both_means = lax.all_gather(grad_mean, "core", axis=0, tiled=True)
    (payload,) = in_vmem(
        pack_kernel,
        "pack",
        [jax.ShapeDtypeStruct((peers, block, width), BF16)],
        (remote_t, grad_mean, chip_t, both_means, grad_pre),
        flops=2 * 3 * half * nodes * width,
        untouched=1,
        sent=(0,),
    )
    returned = exchange(payload, "dom", PEER_ORDER)
    grad_base = back_product(grad_pre, w_self) + grad_mean.astype(F32) + transposed(local_mat, grad_mean)
    shape = jax.ShapeDtypeStruct((n_z, width // LANES, LANES), F32)
    at_hub = jnp.broadcast_to((at_node == hub_rows[0, 0]).astype(F32), (nodes, LANES))
    (hub_z,) = in_vmem(arrive_kernel, "arrive", [shape], (returned, grad_base), flops=half * width, untouched=1)
    hub_parts = exchange(hub_z, "z", Z_ORDER)

    wide = jnp.concatenate([picked, jnp.full((peers, n_z), -1, jnp.int32)], axis=1)
    wide_pick = (wide.reshape(1, peers * block) == at_node).astype(BF16)
    (grad_local,) = in_vmem(
        tail_kernel,
        "tail",
        [rows_f32],
        (wide_pick, returned, grad_base, at_hub),
        flops=2 * nodes * peers * block * width,
        untouched=1,
    )
    grad_features, hub_grad = in_vmem(
        last_kernel,
        "last",
        [rows_b16, jax.ShapeDtypeStruct((1, width), F32)],
        (grad_local, at_hub, hub_parts),
        flops=nodes * width,
        sent=(0, 1),
    )
    return (out_feats, grad_features, hub_grad)


def solution(mesh):
    fine = Mesh(mesh.devices.reshape(8, CORES, PEERS), ALL)
    rows, whole = P(ALL), P()
    return jax.shard_map(
        on_device,
        mesh=fine,
        in_specs=(rows, whole, whole, whole, rows, rows, rows, rows, rows, rows, rows, rows),
        out_specs=(rows, rows, rows),
        check_vma=False,
    )
```

```python
import jax
import jax.numpy as jnp
from jax import lax
from jax.experimental import pallas as pl
from jax.experimental.pallas import tpu as pltpu
from jax.sharding import Mesh
from jax.sharding import PartitionSpec as P

ALL = ("z", "core", "dom")
F32 = jnp.float32
BF16 = jnp.bfloat16
LANES = 128
ROWS = 16
CORES, PEERS = 2, 32


def peer_at(place):
    place = (place + 19) & (PEERS - 1)
    return ((place & 3) << 3) | (place >> 2)


PEER_ORDER = [peer_at(k) for k in range(PEERS)]
PEER_PLACE = [PEER_ORDER.index(k) for k in range(PEERS)]
Z_ORDER = [4, 5, 6, 7, 0, 1, 2, 3]


def taken(blocks, places):
    return jnp.concatenate([blocks[k : k + 1] for k in places], axis=0)


def matmul(lhs, rhs):
    return jnp.dot(lhs, rhs, preferred_element_type=F32)


def transposed(matrix, other):
    return lax.dot_general(matrix, other, (((0,), (0,)), ((), ())), preferred_element_type=F32)


def back_product(grads, weight):
    return lax.dot_general(grads, weight, (((1,), (1,)), ((), ())), preferred_element_type=F32)


def exchange(parts, axis, order=None):
    groups = None if order is None else [order]
    return lax.all_to_all(parts, axis, split_axis=0, concat_axis=0, tiled=True, axis_index_groups=groups)


def split_lanes(rows):
    parts = [rows[:, k : k + LANES] for k in range(0, rows.shape[1], LANES)]
    return jnp.stack(parts, axis=1)


def in_vmem(body, name, shapes, operands, flops, limit=8, untouched=0, sent=()):
    spec, anywhere = pl.BlockSpec(memory_space=pltpu.VMEM), pl.BlockSpec(memory_space=pltpu.HBM)
    moved = sum(x.size * x.dtype.itemsize for x in (*operands, *shapes)) if flops else 0
    scratch = [pltpu.VMEM(shapes[k].shape, shapes[k].dtype) for k in sent]
    return pl.pallas_call(
        body,
        out_shape=shapes,
        in_specs=[spec] * (len(operands) - untouched) + [pl.BlockSpec(memory_space=pl.ANY)] * untouched,
        out_specs=[anywhere if k in sent else spec for k in range(len(shapes))],
        scratch_shapes=scratch + [pltpu.SemaphoreType.DMA((2,))] if sent else [],
        compiler_params=pltpu.CompilerParams(vmem_limit_bytes=limit * 1024 * 1024),
        cost_estimate=pl.CostEstimate(flops=flops, bytes_accessed=moved, transcendentals=0),
        name=name,
    )(*operands)


def in_halves(out_ref, held, sem, value):
    half = out_ref.shape[-1] // 2
    copies = []
    for k in range(2):
        columns = slice(k * half, (k + 1) * half)
        held[..., columns] = value(columns)
        copies.append(pltpu.make_async_copy(held.at[..., columns], out_ref.at[..., columns], sem.at[k]))
        copies[k].start()
    for copy in copies:
        copy.wait()


def hub_row_kernel(place_ref, rows_ref, out_ref, block, sem):
    row = place_ref[0, 0]
    first = pl.multiple_of(row // ROWS * ROWS, ROWS)
    copy = pltpu.make_async_copy(rows_ref.at[pl.ds(first, ROWS)], block, sem)
    copy.start()
    copy.wait()
    at = lax.broadcasted_iota(jnp.int32, block.shape, 0) == row - first
    own = jnp.sum(jnp.where(at, block[...].astype(F32), 0.0), axis=0, keepdims=True)
    out_ref[...] = jnp.broadcast_to(split_lanes(own), out_ref.shape)


def hub_row(hub_rows, features, n_z):
    width = features.shape[1]
    return pl.pallas_call(
        hub_row_kernel,
        out_shape=jax.ShapeDtypeStruct((n_z, width // LANES, LANES), F32),
        in_specs=[pl.BlockSpec(memory_space=pltpu.SMEM), pl.BlockSpec(memory_space=pl.ANY)],
        out_specs=pl.BlockSpec(memory_space=pltpu.VMEM),
        scratch_shapes=[pltpu.VMEM((ROWS, width), BF16), pltpu.SemaphoreType.DMA],
        compiler_params=pltpu.CompilerParams(vmem_limit_bytes=60 * 1024 * 1024),
        name="hub_row",
    )(hub_rows, features)


def payload_kernel(along_z, outgoing, base, base_pre, out_ref, held, sem):
    del base, base_pre
    peers = out_ref.shape[0]

    def value(columns):
        parts = [along_z[:, k // LANES, :] for k in range(columns.start, columns.stop, LANES)]
        hubs = jnp.concatenate(parts, axis=1)
        hubs = jnp.broadcast_to(hubs[None], (peers, *hubs.shape))
        slots = outgoing[:, columns].astype(F32).reshape(peers, -1, hubs.shape[2])
        return jnp.concatenate([taken(slots, PEER_ORDER), hubs], axis=1).astype(BF16)

    in_halves(out_ref, held, sem, value)


def adjacency_kernel(hub_adj, remote_adj, hub_mat, hub_t, remote_mat, remote_t):
    hubs, slots = hub_t.shape[0], remote_t.shape[0]
    n_z = hubs // (CORES * PEERS)
    shift = n_z.bit_length() - 1

    def source(place):
        at_core, at_peer, at_z = place >> shift + 5, (place >> shift) & (PEERS - 1), place & (n_z - 1)
        return (at_z * CORES + at_core) * PEERS + peer_at(at_peer)

    column = lax.broadcasted_iota(jnp.int32, (hubs, 1), 0)
    row = lax.broadcasted_iota(jnp.int32, (1, hubs), 1)
    hub_rows = hub_adj[...].astype(BF16)
    hub_mat[...] = matmul(hub_rows, (source(row) == column).astype(BF16)).astype(BF16)
    hub_t[...] = back_product((source(column) == row).astype(BF16), hub_rows).astype(BF16)
    remote_rows = remote_adj[...].astype(BF16)
    remote_mat[...] = remote_rows
    same = (column[:slots] == row[:, :slots]).astype(BF16)
    remote_t[...] = back_product(same, remote_rows).astype(BF16)


def middle_kernel(
    hubs, hub_mat, incoming, remote_mat, base, inverse, weight, base_pre, grad, out_ref, pre_ref, mean_ref, out, pre, sem
):
    peers, width = incoming.shape[0], incoming.shape[2]
    received = incoming[...].astype(F32)[:, : remote_mat.shape[1] // peers]
    received = taken(received, PEER_PLACE).reshape(remote_mat.shape[1], width).astype(BF16)
    total = matmul(hub_mat[...], hubs[...]) + matmul(remote_mat[...], received)
    scale = jnp.concatenate([inverse[...]] * (total.shape[1] // LANES), axis=1)
    mean_feats = ((total + base[...]) * scale).astype(BF16)
    preact = matmul(mean_feats, weight[...]) + base_pre[...]
    low = jnp.minimum(preact, 0.0)
    grown = jnp.exp(low)
    near = low * (1.0 + low * (0.5 + low * (1.0 / 6.0)))
    below = jnp.where(low > -0.02, near, grown - 1.0)
    out[...] = jnp.where(preact > 0, preact, below).astype(BF16)
    grad_pre = (grad[...].astype(F32) * grown).astype(BF16)
    pre[...] = grad_pre
    copies = [pltpu.make_async_copy(*pair, sem.at[k]) for k, pair in enumerate(((out, out_ref), (pre, pre_ref)))]
    for copy in copies:
        copy.start()
    mean_ref[...] = (back_product(grad_pre, weight[...]) * scale).astype(BF16)
    for copy in copies:
        copy.wait()


def pack_kernel(remote_t, grad_mean, hub_t, both_means, grad_pre, out_ref, held, sem):
    del grad_pre
    peers, nodes = out_ref.shape[0], grad_mean.shape[0]

    def value(columns):
        slots = matmul(remote_t[...], grad_mean[:, columns])
        hubs = matmul(hub_t[0], both_means[:nodes, columns]) + matmul(hub_t[1], both_means[nodes:, columns])
        slots, hubs = (x.reshape(peers, -1, x.shape[1]) for x in (slots, hubs))
        return jnp.concatenate([taken(slots, PEER_ORDER), hubs], axis=1).astype(BF16)

    in_halves(out_ref, held, sem, value)


def arrive_kernel(returned, base, out_ref):
    del base
    total = jnp.sum(returned[...].astype(F32), axis=0)
    out_ref[...] = taken(split_lanes(total[total.shape[0] - out_ref.shape[0] :]), Z_ORDER)


def tail_kernel(pick, returned, base, at_hub, out_ref):
    del at_hub
    blocks = taken(returned[...], PEER_PLACE)
    out_ref[...] = base[...] + matmul(pick[...], blocks.reshape(-1, blocks.shape[2]))


def last_kernel(grad_local, at_hub, parts, out_ref, hub_ref, held, held_hub, sem):
    total = jnp.sum(parts[...], axis=0)
    hub = jnp.concatenate([total[k : k + 1] for k in range(total.shape[0])], axis=1)
    held_hub[...] = hub
    here = jnp.concatenate([at_hub[...]] * total.shape[0], axis=1) > 0
    held[...] = (grad_local[...] + jnp.where(here, hub, 0.0)).astype(BF16)
    copies = [pltpu.make_async_copy(*pair, sem.at[k]) for k, pair in enumerate(((held, out_ref), (held_hub, hub_ref)))]
    for copy in copies:
        copy.start()
    for copy in copies:
        copy.wait()


def on_device(
    features,
    w_self,
    w_neigh,
    bias_term,
    degree,
    local_adj,
    hub_adj,
    hub_rows,
    remote_adj,
    send_rows,
    send_counts,
    grad_out,
):
    nodes, width = features.shape
    n_z, n_core = lax.axis_size("z"), lax.axis_size("core")
    peers, slots = send_rows.shape[1:]
    hubs = hub_adj.shape[1]
    half = hubs // n_core
    block = slots + n_z
    first_core = lax.axis_index("core") == 0
    rows_f32 = jax.ShapeDtypeStruct((nodes, width), F32)
    rows_b16 = jax.ShapeDtypeStruct((nodes, width), BF16)

    along_z = exchange(hub_row(hub_rows, features, n_z), "z")

    live = jnp.arange(slots, dtype=jnp.int32)[None, :] < send_counts[0][:, None]
    picked = jnp.where(live, send_rows[0], -1)
    at_node = jnp.arange(nodes, dtype=jnp.int32)[:, None]
    pick = (picked.reshape(1, peers * slots) == at_node).astype(BF16)
    outgoing = transposed(pick, features).astype(BF16)
    local_mat = local_adj.astype(BF16)
    base = features.astype(F32) + matmul(local_mat, features)
    base_pre = matmul(features, w_self) + bias_term
    (payload,) = in_vmem(
        payload_kernel,
        "payload",
        [jax.ShapeDtypeStruct((peers, block, width), BF16)],
        (along_z, outgoing, base, base_pre),
        flops=peers * block * width,
        untouched=2,
        sent=(0,),
    )
    incoming = exchange(payload, "dom", PEER_ORDER)
    same_core = incoming[:, slots:].reshape(half, width)
    all_hubs = lax.all_gather(same_core, "core", axis=0, tiled=True)

    hub_mat, hub_t, remote_mat, remote_t = in_vmem(
        adjacency_kernel,
        "adjacency",
        [jax.ShapeDtypeStruct(shape, BF16) for shape in ((nodes, hubs), (hubs, nodes), (nodes, peers * slots), (peers * slots, nodes))],
        (hub_adj, remote_adj),
        flops=0,
        limit=56,
    )
    chip_t = lax.all_gather(hub_t, "core", axis=0).reshape(n_core, n_core, half, nodes)
    chip_t = jnp.where(first_core, chip_t[:, 0], chip_t[:, 1])

    inverse = jnp.broadcast_to(1.0 / (degree.astype(F32)[:, None] + 1.0), (nodes, LANES))
    out_feats, grad_pre, grad_mean = in_vmem(
        middle_kernel,
        "middle",
        [rows_b16] * 3,
        (all_hubs, hub_mat, incoming, remote_mat, base, inverse, w_neigh, base_pre, grad_out),
        flops=2 * nodes * width * (hubs + peers * slots + 2 * width),
        sent=(0, 1),
    )

    both_means = lax.all_gather(grad_mean, "core", axis=0, tiled=True)
    (payload,) = in_vmem(
        pack_kernel,
        "pack",
        [jax.ShapeDtypeStruct((peers, block, width), BF16)],
        (remote_t, grad_mean, chip_t, both_means, grad_pre),
        flops=2 * 3 * half * nodes * width,
        untouched=1,
        sent=(0,),
    )
    returned = exchange(payload, "dom", PEER_ORDER)
    grad_base = back_product(grad_pre, w_self) + grad_mean.astype(F32) + transposed(local_mat, grad_mean)
    shape = jax.ShapeDtypeStruct((n_z, width // LANES, LANES), F32)
    at_hub = jnp.broadcast_to((at_node == hub_rows[0, 0]).astype(F32), (nodes, LANES))
    (hub_z,) = in_vmem(arrive_kernel, "arrive", [shape], (returned, grad_base), flops=half * width, untouched=1)
    hub_parts = exchange(hub_z, "z", Z_ORDER)

    wide = jnp.concatenate([picked, jnp.full((peers, n_z), -1, jnp.int32)], axis=1)
    wide_pick = (wide.reshape(1, peers * block) == at_node).astype(BF16)
    (grad_local,) = in_vmem(
        tail_kernel,
        "tail",
        [rows_f32],
        (wide_pick, returned, grad_base, at_hub),
        flops=2 * nodes * peers * block * width,
        untouched=1,
    )
    grad_features, hub_grad = in_vmem(
        last_kernel,
        "last",
        [rows_b16, jax.ShapeDtypeStruct((1, width), F32)],
        (grad_local, at_hub, hub_parts),
        flops=nodes * width,
        sent=(0, 1),
    )
    return (out_feats, grad_features, hub_grad)


def solution(mesh):
    fine = Mesh(mesh.devices.reshape(8, CORES, PEERS), ALL)
    rows, whole = P(ALL), P()
    return jax.shard_map(
        on_device,
        mesh=fine,
        in_specs=(rows, whole, whole, whole, rows, rows, rows, rows, rows, rows, rows, rows),
        out_specs=(rows, rows, rows),
        check_vma=False,
    )
```
